512 devices in a mesh: chan: 64 (over x, z_lo, y), tile: 4 (over z_hi), cores: 2 (over core).
Axes of the slice: x: 4, y: 8, z: 8 (z_hi: 4, z_lo: 2; z = z_hi * 2 + z_lo), core: 2. Of those that a mesh axis runs over, the one named last changes fastest.
Arguments:
- samples: bfloat16 [8, 256, 131840], P(('tile', 'cores'), 'chan'), may hold values from -6 to 6
- filter_taps: float32 [4, 256], replicated, may hold values from -3 to 3
- kept_channels: int32 [64], replicated, may hold values from 0 to 255
- input_flags: int32 [8, 256], P(('tile', 'cores'), 'chan'), may hold values 0 or 1
Outputs:
- visibilities: float32 [64, 2, 2048, 2048], P('chan', None, ('tile', 'cores'))
The draws below stay inside these ranges and needn't reach their ends.
All inputs are finite; a program needn't handle non-finite values. No bound on the sum of `input_flags` on one device may be relied on, other than what follows from the above.
Results may differ from the reference program's by a relative error of at most 0.0035.
Values may be sent and summed in bfloat16 or wider, within the bound.
A program may use at most 64 MiB of HBM per device.

```python
import math
import jax
import jax.numpy as jnp
from jax import lax

INPUTS = 2048
POINTS = 256
TAPS = 4
SPECTRA = 512
CHANS = 64
BLOCKS = 8
GROUP = 256
SAMPLES = 131840


def plant(drawn, stream_key, least, high):
    longest = drawn.shape.index(max(drawn.shape))
    spots = []
    for shift in (0, 1):
        where = [jax.random.randint(jax.random.fold_in(stream_key, axis), (), 0, length) for axis, length in enumerate(drawn.shape)]
        where[longest] = (where[longest] + shift) % drawn.shape[longest]
        spots.append(tuple(where))
    return drawn.at[spots[0]].set(least).at[spots[1]].set(high)


def level_of(own_key, shape, cuts, low, top_value):
    def one(dim, blocks):
        heights = jax.random.uniform(jax.random.fold_in(jax.random.fold_in(own_key, 6), dim), (blocks,), jnp.float32, low / len(cuts), top_value / len(cuts))
        return jnp.repeat(jnp.exp(heights), shape[dim] // blocks).reshape((-1,) + (1,) * (len(shape) - dim - 1))

    gain = one(*cuts[0])
    for cut in cuts[1:]:
        gain = gain * one(*cut)
    return gain


def scatter_about(key, shape, width, limit, shards=(), held_as=jnp.bfloat16):
    drawn = width * jax.random.normal(key, shape, jnp.float32)
    if shards:
        drawn = drawn * level_of(key, shape, shards, -0.22, 0.18)
    return jnp.clip(drawn, -limit, limit).astype(held_as)


def setup_inputs(seed: int = 0) -> dict:
    keys = jax.random.split(jax.random.key(seed), 5)
    return {
        "samples": scatter_about(keys[0], (BLOCKS, GROUP, SAMPLES), 1.0, 6.0, ((0, 8), (1, 64))),
        "filter_taps": scatter_about(keys[1], (TAPS, POINTS), 0.5, 3.0, (), jnp.float32),
        "kept_channels": plant(jax.random.randint(keys[2], (CHANS,), 0, POINTS), jax.random.fold_in(keys[2], 1), 0, POINTS - 1).astype(jnp.int32),
        "input_flags": plant((jax.random.randint(keys[3], (BLOCKS, GROUP), 0, 8) < 7).astype(jnp.int32), jax.random.fold_in(keys[3], 1), 0, 1),
    }


def dft_table(kept_channels, points):
    index = jnp.arange(points, dtype=jnp.int32)
    product = kept_channels[:, None].astype(jnp.int32) * index[None, :] % points
    phase = product.astype(jnp.float32) * (2.0 * math.pi / points)
    scaled = 1.0 / math.sqrt(points)
    table = jnp.stack([jnp.cos(phase) * scaled, -jnp.sin(phase) * scaled], axis=1)
    return table.reshape(2 * kept_channels.shape[0], points)

def reference(samples, filter_taps, kept_channels, input_flags):
    table = dft_table(kept_channels, POINTS)

    def front(block):
        block_samples, block_flags = block
        frames = block_samples.reshape(GROUP, SPECTRA + TAPS - 1, POINTS)
        filtered = filter_taps[0][None, None, :] * frames[:, 0:SPECTRA, :].astype(jnp.float32)
        for step in range(1, TAPS):
            filtered = filtered + filter_taps[step][None, None, :] * frames[:, step:step + SPECTRA, :].astype(jnp.float32)
        spectrum = jnp.einsum('rp,isp->ris', table, filtered, precision=lax.Precision.HIGHEST)
        spectrum = spectrum * block_flags.astype(jnp.float32)[None, :, None]
        return spectrum.astype(jnp.bfloat16)
    spectra_all = lax.map(front, (samples, input_flags))
    spectra_all = jnp.transpose(spectra_all, (1, 0, 2, 3)).reshape(CHANS, 2, INPUTS, SPECTRA)

    def outer(left, right):
        return jnp.dot(left, right.T, preferred_element_type=jnp.float32)

    def correlate(channel):
        real_part = channel[0]
        imag_part = channel[1]
        real_out = outer(real_part, real_part) + outer(imag_part, imag_part)
        imag_out = outer(imag_part, real_part) - outer(real_part, imag_part)
        return jnp.stack([real_out, imag_out]) * (1.0 / SPECTRA)
    return lax.map(correlate, spectra_all)
```

```python
import functools
import math

import jax
import jax.numpy as jnp
import numpy as np
from jax import lax
from jax.experimental import pallas as pl
from jax.experimental.pallas import tpu as pltpu
from jax.sharding import PartitionSpec as P

MESH = pl.DeviceIdType.MESH
F32, BF16 = jnp.float32, jnp.bfloat16
NX, NY, NZ = 4, 8, 8
CH = 4
NT = (((1,), (1,)), ((), ()))


def place():
    chan, tile, core = lax.axis_index("chan"), lax.axis_index("tile"), lax.axis_index("cores")
    return chan // (2 * NY), chan % NY, tile * 2 + (chan // NY) % 2, core


def device(x, y, z, core):
    x, y, z = x % NX, y % NY, z % NZ
    return ((x * 2 + z % 2) * NY + y, z // 2, core)


def twiddles(points):
    phase = (np.outer(np.arange(points), np.arange(points)) % points) * (2.0 * math.pi / points)
    whole = np.concatenate([np.cos(phase), -np.sin(phase)], axis=1) / math.sqrt(points)
    whole = whole.astype(np.float32)
    high = whole.astype(BF16)
    low = (whole - high.astype(np.float32)).astype(BF16)
    return np.stack([high, low])


def channel_rows():
    rows = np.zeros((2 * NX * 2 * NY, NX * 2 * NY), np.float32)
    for yc in range(NY):
        for xc in range(NX):
            for zl in range(2):
                for q in range(2):
                    rows[((yc * NX + xc) * 2 + zl) * 2 + q, (xc * 2 + zl) * NY + yc] = 1.0
    return rows.astype(BF16)


def spectra_kernel(samples, taps, kept, flags, twiddle, select, out, table, wide):
    points = taps.shape[1]
    blocks = samples.shape[2] // 128
    inputs = samples.shape[1]
    chosen = (lax.broadcasted_iota(jnp.int32, (points, kept.shape[1]), 0) == kept[...]).astype(F32).astype(BF16)
    onehot = lax.dot_general(select[...], chosen, NT, preferred_element_type=F32).astype(BF16)
    odd = lax.broadcasted_iota(jnp.int32, (onehot.shape[0], points), 0) % 2 == 1
    for part in range(2):
        both = jnp.dot(onehot, twiddle[part], preferred_element_type=F32)
        table[part] = jnp.where(odd, both[:, points:], both[:, :points]).astype(BF16)

    unroll = 10

    def widen(step, _):
        for u in range(unroll):
            block = step * unroll + u
            piece = samples[0, :, pl.ds(pl.multiple_of(block * 128, 128), 128)].astype(F32)
            wide[pl.ds(pl.multiple_of(block * inputs, inputs), inputs), :] = piece
        return 0

    lax.fori_loop(0, blocks // unroll, widen, 0)
    stride = 2 * inputs

    def chunk(h, _):
        for i in range(inputs):
            halves = []
            for half in range(2):
                total = None
                for t in range(taps.shape[0]):
                    rows = wide[pl.ds((h * 128 + t) * stride + half * inputs + i, 128, stride=stride), :]
                    term = taps[pl.ds(t, 1), pl.ds(half * 128, 128)] * rows
                    total = term if total is None else total + term
                halves.append(total)
            filtered = jnp.concatenate(halves, axis=1)
            high = filtered.astype(BF16)
            low = (filtered - high.astype(F32)).astype(BF16)
            spectrum = lax.dot_general(table[0], high, NT, preferred_element_type=F32)
            spectrum += lax.dot_general(table[0], low, NT, preferred_element_type=F32)
            spectrum += lax.dot_general(table[1], high, NT, preferred_element_type=F32)
            spectrum = spectrum * flags[0, i].astype(F32)
            out[h, :, i] = spectrum.astype(BF16).reshape(out.shape[1], out.shape[3], 128)
        return 0

    lax.fori_loop(0, CH, chunk, 0)


def turn_kernel(spec, out, yr, wide, xs, held, ysend, yrecv, xsend, xrecv, zsend, zrecv, csend, crecv, own):
    x, y, z, k = place()
    sib = device(x, y, z, 1 - k)
    barrier = pltpu.get_barrier_semaphore()
    partners = [device(x, y + d, z, k) for d in range(1, NY)]
    partners += [device(x + d, y, z, k) for d in range(1, NX)]
    partners += [device(x, y, z + d, k) for d in (1, 2, NZ - 1, NZ - 2)] + [sib]
    for d in partners:
        pl.semaphore_signal(barrier, inc=1, device_id=d, device_id_type=MESH)
    pl.semaphore_wait(barrier, len(partners))

    def remote(src, dst, ssem, rsem, dev):
        pltpu.make_async_remote_copy(
            src_ref=src, dst_ref=dst, send_sem=ssem, recv_sem=rsem, device_id=dev, device_id_type=MESH
        ).start()

    def wait(ref, sem):
        pltpu.make_async_copy(ref, ref, sem).wait()

    def slot(h, d):
        src = (z + d) % NZ
        return out.at[h, (src // 2) * 2 + k, src % 2]

    def send_y(h):
        pltpu.make_async_copy(spec.at[h, y], yr.at[h, y], yrecv.at[h]).start()
        for d in (4, 3, 5, 2, 6, 1, 7):
            to = (y + d) % NY
            remote(spec.at[h, to], yr.at[h, y], ysend, yrecv.at[h], device(x, y + d, z, k))

    def turn(h):
        wide[...] = yr[h].reshape(wide.shape).astype(F32)
        for r in range(16):
            rows = wide[pl.ds(r, 32, stride=16), :]
            xs[h, r // 4, (r // 2) % 2, r % 2] = rows.astype(BF16)

    def send_x(h):
        pltpu.make_async_copy(xs.at[h, x], held.at[h, x], xrecv.at[h]).start()
        for d in (2, 1, 3):
            to = (x + d) % NX
            remote(xs.at[h, to], held.at[h, x], xsend, xrecv.at[h], device(x + d, y, z, k))

    def forward(h, d):
        remote(slot(h, d), slot(h, d), csend, crecv, sib)

    def send_z(h):
        same, other = held.at[h, :, z % 2], held.at[h, :, 1 - z % 2]
        remote(same, slot(h, 0), zsend, zrecv.at[h, 2], device(x, y, z + 2, k))
        remote(same, slot(h, 0), zsend, zrecv.at[h, 3], device(x, y, z - 2, k))
        remote(other, slot(h, 0), zsend, zrecv.at[h, 0], device(x, y, z + 1, k))
        remote(other, slot(h, 0), zsend, zrecv.at[h, 1], device(x, y, z - 1, k))
        pltpu.make_async_copy(same, slot(h, 0), own).start()
        remote(same, slot(h, 0), csend, crecv, sib)

    def relay_z(h):
        sign = 1 - 2 * ((h + k) % 2)
        wait(slot(h, -1), zrecv.at[h, 0])
        remote(slot(h, -1), slot(h, -1), zsend, zrecv.at[h, 4], device(x, y, z + 2, k))
        wait(slot(h, 1), zrecv.at[h, 1])
        remote(slot(h, 1), slot(h, 1), zsend, zrecv.at[h, 5], device(x, y, z - 2, k))
        wait(slot(h, -2), zrecv.at[h, 2])
        wait(slot(h, 2), zrecv.at[h, 3])
        remote(slot(h, -2 * sign), slot(h, -2 * sign), zsend, zrecv.at[h, 6], device(x, y, z + 2 * sign, k))
        for d in (-1, 1, -2, 2):
            forward(h, d)

    def finish_z(h):
        wait(slot(h, -3), zrecv.at[h, 4])
        forward(h, -3)
        wait(slot(h, 3), zrecv.at[h, 5])
        forward(h, 3)
        wait(slot(h, 4), zrecv.at[h, 6])
        forward(h, 4)

    send_y(0)
    for h in range(CH):
        wait(yr.at[h], yrecv.at[h])
        if h + 1 < CH:
            send_y(h + 1)
        turn(h)
        send_x(h)
        wait(held.at[h], xrecv.at[h])
        send_z(h)
        if h >= 1:
            relay_z(h - 1)
        if h >= 2:
            finish_z(h - 2)
    relay_z(CH - 1)
    finish_z(CH - 2)
    finish_z(CH - 1)

    wait(out.at[:, pl.ds(0, 4)], crecv)
    wait(out.at[:, pl.ds(0, 4)], csend)
    wait(spec.at[:, pl.ds(0, NY - 1)], ysend)
    wait(xs.at[:, pl.ds(0, NX - 1)], xsend)
    wait(out.at[:, pl.ds(0, 7), 0], zsend)
    wait(out.at[:, 0, 0], own)


def correlate_kernel(scale, spectra, own_hbm, out, own, left, right, sem):
    step = pl.program_id(0)
    rows = out.shape[2]

    def lay(block, h, q):
        pieces = [block[h, zl, xx, q] for xx in range(NX) for zl in range(2)]
        return jnp.concatenate(pieces, axis=0)

    @pl.when(step == 0)
    def _():
        mine = lax.axis_index("tile") * 2 + lax.axis_index("cores")
        copy = pltpu.make_async_copy(own_hbm.at[:, mine], own, sem)
        copy.start()
        copy.wait()
        for h in range(CH):
            for q in range(2):
                block = lay(own, h, q)
                left[pl.ds(0, rows), pl.ds((h * 2 + q) * 128, 128)] = block
                left[pl.ds(rows, rows), pl.ds((h * 2 + 1 - q) * 128, 128)] = block if q else -block

    for h in range(CH):
        for q in range(2):
            right[:, pl.ds((h * 2 + q) * 128, 128)] = lay(spectra.at[:, 0], h, q)
    block = lax.dot_general(left[...], right[...], NT, preferred_element_type=F32) * scale
    out[0] = block.reshape(2, rows, block.shape[1])


def per_device(samples, filter_taps, kept_channels, input_flags):
    taps, points = filter_taps.shape
    inputs, length = samples.shape[1:]
    frames = length // points
    count = frames - taps + 1
    channels = kept_channels.shape[0]
    vmem, hbm = pl.BlockSpec(memory_space=pltpu.VMEM), pl.BlockSpec(memory_space=pl.ANY)
    dma = pltpu.SemaphoreType.DMA

    spec = pl.pallas_call(
        spectra_kernel,
        out_shape=jax.ShapeDtypeStruct((CH, NY, inputs, 2 * channels // NY, 128), BF16),
        in_specs=[vmem, vmem, vmem, pl.BlockSpec(memory_space=pltpu.SMEM), vmem, vmem],
        out_specs=vmem,
        scratch_shapes=[
            pltpu.VMEM((2, 2 * channels, points), BF16),
            pltpu.VMEM((length // 128 * inputs, 128), F32),
        ],
        compiler_params=pltpu.CompilerParams(vmem_limit_bytes=32 << 20),
        name="spectra",
    )(
        samples,
        filter_taps,
        kept_channels.reshape(1, channels),
        input_flags,
        jnp.asarray(twiddles(points)),
        jnp.asarray(channel_rows()),
    )

    gathered = pl.pallas_call(
        turn_kernel,
        out_shape=jax.ShapeDtypeStruct((CH, 8, 2, NX, 2, 32, 128), BF16),
        in_specs=[hbm],
        out_specs=hbm,
        scratch_shapes=[
            pltpu.VMEM((CH, NY, inputs, 16, 128), BF16),
            pltpu.VMEM((NY * inputs * 16, 128), F32),
            pltpu.VMEM((CH, NX, 2, 2, 32, 128), BF16),
            pltpu.VMEM((CH, NX, 2, 2, 32, 128), BF16),
            dma,
            dma((CH,)),
            dma,
            dma((CH,)),
            dma,
            dma((CH, 7)),
            dma,
            dma,
            dma,
        ],
        compiler_params=pltpu.CompilerParams(
            collective_id=0, has_side_effects=True, vmem_limit_bytes=32 << 20
        ),
        name="turn",
    )(spec)

    rows = 256
    return pl.pallas_call(
        functools.partial(correlate_kernel, 1.0 / count),
        grid=(8,),
        out_shape=jax.ShapeDtypeStruct((1, 2, rows, 8 * rows), F32),
        in_specs=[pl.BlockSpec((CH, 1, 2, NX, 2, 32, 128), lambda b: (0, b, 0, 0, 0, 0, 0)), hbm],
        out_specs=pl.BlockSpec((1, 2, rows, rows), lambda b: (0, 0, 0, b)),
        scratch_shapes=[
            pltpu.VMEM((CH, 2, NX, 2, 32, 128), BF16),
            pltpu.VMEM((2 * rows, 2 * count), BF16),
            pltpu.VMEM((rows, 2 * count), BF16),
            dma,
        ],
        compiler_params=pltpu.CompilerParams(vmem_limit_bytes=32 << 20),
        name="correlate",
    )(gathered, gathered)


def solution(mesh):
    in_specs = (P(("tile", "cores"), "chan", None), P(), P(), P(("tile", "cores"), "chan"))
    out_specs = P("chan", None, ("tile", "cores"), None)
    return jax.shard_map(
        per_device, mesh=mesh, in_specs=in_specs, out_specs=out_specs, check_vma=False
    )
```

```python
import functools
import math

import jax
import jax.numpy as jnp
import numpy as np
from jax import lax
from jax.experimental import pallas as pl
from jax.experimental.pallas import tpu as pltpu
from jax.sharding import PartitionSpec as P

MESH = pl.DeviceIdType.MESH
F32, BF16 = jnp.float32, jnp.bfloat16
NX, NY, NZ = 4, 8, 8
CH = 4
NT = (((1,), (1,)), ((), ()))
REL = (0, -1, 1, -2, 2, -3, 3, 4)


def place():
    chan, tile, core = lax.axis_index("chan"), lax.axis_index("tile"), lax.axis_index("cores")
    return chan // (2 * NY), chan % NY, tile * 2 + (chan // NY) % 2, core


def device(x, y, z, core):
    x, y, z = x % NX, y % NY, z % NZ
    return ((x * 2 + z % 2) * NY + y, z // 2, core)


def twiddles(points):
    phase = (np.outer(np.arange(points), np.arange(points)) % points) * (2.0 * math.pi / points)
    whole = np.concatenate([np.cos(phase), -np.sin(phase)], axis=1) / math.sqrt(points)
    whole = whole.astype(np.float32)
    high = whole.astype(BF16)
    low = (whole - high.astype(np.float32)).astype(BF16)
    return np.stack([high, low])


def body(
    scale, samples_hbm, taps_hbm, kept_hbm, flags_hbm, twiddle_hbm, vis,
    samples, taps, kept, flags, twiddle, table, wide, first, spec, yr, turned, xs, held, za, zb, zx, got, left,
    load, ysend, yrecv, xsend, xrecv, zsend, zrecv, csend, crecv, own, y0send, y0recv, x0send, x0recv,
):
    x, y, z, k = place()
    points = taps.shape[1]
    inputs = samples.shape[1]
    chunk_blocks, extra = 256, 2 * (taps.shape[0] - 1)

    def wait(ref, sem):
        pltpu.make_async_copy(ref, ref, sem).wait()

    def remote(src, dst, ssem, rsem, dev):
        pltpu.make_async_remote_copy(
            src_ref=src, dst_ref=dst, send_sem=ssem, recv_sem=rsem, device_id=dev, device_id_type=MESH
        ).start()

    def part(h):
        start = 0 if h == 0 else h * chunk_blocks + extra
        size = chunk_blocks + (extra if h == 0 else 0)
        return start, size

    def piece(h):
        start, size = part(h)
        return pl.ds(start * 128, size * 128)

    small = [(kept_hbm, kept), (twiddle_hbm, twiddle), (taps_hbm, taps), (flags_hbm, flags)]
    loads = [pltpu.make_async_copy(src, dst, load.at[CH + n]) for n, (src, dst) in enumerate(small)]
    for h in range(CH):
        loads.append(
            pltpu.make_async_copy(samples_hbm.at[:, :, piece(h)], samples.at[:, :, piece(h)], load.at[h])
        )
    for copy in loads:
        copy.start()

    sib = device(x, y, z, 1 - k)
    barrier = pltpu.get_barrier_semaphore()
    partners = [device(x, y + d, z, k) for d in range(1, NY)]
    partners += [device(x + d, y, z, k) for d in range(1, NX)]
    partners += [device(x, y, z + d, k) for d in (1, 2, NZ - 1, NZ - 2)] + [sib]
    for d in partners:
        pl.semaphore_signal(barrier, inc=1, device_id=d, device_id_type=MESH)

    for copy in loads[:4]:
        copy.wait()
    chosen = (lax.broadcasted_iota(jnp.int32, (points, kept.shape[1]), 0) == kept[...]).astype(F32).astype(BF16)
    row = lax.broadcasted_iota(jnp.int32, (table.shape[2], kept.shape[1]), 0)
    column = lax.broadcasted_iota(jnp.int32, row.shape, 1)
    orders = (
        (((row >> 1) & 3) * 2 + (row >> 6)) * NY + ((row >> 3) & 7),
        ((row >> 1) & 7) * NY + (row >> 4),
    )
    odd = lax.broadcasted_iota(jnp.int32, (table.shape[2], points), 0) % 2 == 1
    for n, order in enumerate(orders):
        select = (order == column).astype(F32).astype(BF16)
        onehot = lax.dot_general(select, chosen, NT, preferred_element_type=F32).astype(BF16)
        for p in range(2):
            both = jnp.dot(onehot, twiddle[p], preferred_element_type=F32)
            table[n, p] = jnp.where(odd, both[:, points:], both[:, :points]).astype(BF16)

    stride = 2 * inputs

    def widen(h):
        loads[4 + h].wait()
        start, size = part(h)
        unroll = 16 if size % 16 == 0 else 2

        def step(s, _):
            for u in range(unroll):
                block = start + s * unroll + u
                values = samples[0, :, pl.ds(pl.multiple_of(block * 128, 128), 128)].astype(F32)
                wide[pl.ds(pl.multiple_of(block * inputs, inputs), inputs), :] = values
            return 0

        lax.fori_loop(0, size // unroll, step, 0)

    def transform(h, i, n):
        halves = []
        for half in range(2):
            total = None
            for t in range(taps.shape[0]):
                rows = wide[pl.ds((h * 128 + t) * stride + half * inputs + i, 128, stride=stride), :]
                term = taps[pl.ds(t, 1), pl.ds(half * 128, 128)] * rows
                total = term if total is None else total + term
            halves.append(total)
        filtered = jnp.concatenate(halves, axis=1)
        high = filtered.astype(BF16)
        low = (filtered - high.astype(F32)).astype(BF16)
        spectrum = lax.dot_general(table[n, 0], high, NT, preferred_element_type=F32)
        spectrum += lax.dot_general(table[n, 0], low, NT, preferred_element_type=F32)
        spectrum += lax.dot_general(table[n, 1], high, NT, preferred_element_type=F32)
        return spectrum * flags[pl.ds(0, 1), pl.ds(i, 1)].astype(F32)

    def spectra_first():
        widen(0)
        for m in range(inputs // 2):
            pair = [transform(0, 2 * m + i, 0).reshape(2, NY, 8, 128) for i in range(2)]
            first[:, :, m] = jnp.concatenate(pair, axis=2).astype(BF16)

    def spectra(h):
        widen(h)
        for i in range(inputs):
            spec[h - 1, :, i] = transform(h, i, 1).astype(BF16).reshape(NY, 16, 128)

    def send_y(h):
        pltpu.make_async_copy(spec.at[h - 1, y], yr.at[h - 1, y], yrecv.at[h - 1]).start()
        for d in (4, 3, 5, 2, 6, 1, 7):
            to = (y + d) % NY
            remote(spec.at[h - 1, to], yr.at[h - 1, y], ysend, yrecv.at[h - 1], device(x, y + d, z, k))

    def turn(h):
        wait(yr.at[h - 1], yrecv.at[h - 1])
        turned[...] = yr[h - 1].reshape(turned.shape).astype(F32)
        for r in range(16):
            rows = turned[pl.ds(r, 32, stride=16), :]
            xs[h - 1, r // 4, (r // 2) % 2, r % 2] = rows.astype(BF16)

    def send_x(h):
        pltpu.make_async_copy(xs.at[h - 1, x], held.at[h - 1, x], xrecv.at[h - 1]).start()
        for d in (2, 1, 3):
            to = (x + d) % NX
            remote(xs.at[h - 1, to], held.at[h - 1, x], xsend, xrecv.at[h - 1], device(x + d, y, z, k))

    def slot(h, n):
        src = (z + REL[n]) % NZ
        return got.at[h, (src // 2) * 2 + k, src % 2]

    def forward(h, n):
        remote(slot(h, n), slot(h, n), csend, crecv.at[h, n // 5], sib)

    def spread(h, same, other, at):
        remote(same, at(0, 3), zsend, zrecv.at[h, 3], device(x, y, z + 2, k))
        remote(same, at(0, 4), zsend, zrecv.at[h, 4], device(x, y, z - 2, k))
        remote(other, at(0, 1), zsend, zrecv.at[h, 1], device(x, y, z + 1, k))
        remote(other, at(0, 2), zsend, zrecv.at[h, 2], device(x, y, z - 1, k))
        pltpu.make_async_copy(same, at(0, 0), own.at[h]).start()

    def relay(h, at):
        sign = (h + k) % 2
        wait(at(1, 1), zrecv.at[h, 1])
        remote(at(1, 1), at(1, 5), zsend, zrecv.at[h, 5], device(x, y, z + 2, k))
        wait(at(2, 2), zrecv.at[h, 2])
        remote(at(2, 2), at(2, 6), zsend, zrecv.at[h, 6], device(x, y, z - 2, k))
        wait(at(3, 3), zrecv.at[h, 3])
        wait(at(4, 4), zrecv.at[h, 4])
        remote(at(3 + sign, 3 + sign), at(3 + sign, 7), zsend, zrecv.at[h, 7], device(x, y, z + 2 - 4 * sign, k))

    def at_first(_, n):
        return za.at[n]

    def at_slot(h):
        def at(n, _):
            if isinstance(n, int):
                return slot(h, n)
            src = (z - 2 + 4 * (n - 3)) % NZ
            return got.at[h, (src // 2) * 2 + k, src % 2]

        return at

    def send_z(h):
        wait(held.at[h - 1], xrecv.at[h - 1])
        same, other = held.at[h - 1, :, z % 2], held.at[h - 1, :, 1 - z % 2]
        spread(h, same, other, at_slot(h))
        remote(same, slot(h, 0), csend, crecv.at[h, 0], sib)

    def relay_z(h):
        relay(h, at_slot(h))
        for n in range(1, 5):
            forward(h, n)

    def finish_z(h):
        for n in range(5, 8):
            wait(slot(h, n), zrecv.at[h, n])
            forward(h, n)

    groups = ((0, 5), (5, 3))

    def send_y0(g):
        begin, size = groups[g]
        mine = pl.ds(begin, size)
        pltpu.make_async_copy(za.at[mine, y], zb.at[y, mine], y0recv.at[g]).start()
        for d in (4, 3, 5, 2, 6, 1, 7):
            to = (y + d) % NY
            remote(za.at[mine, to], zb.at[y, mine], y0send, y0recv.at[g], device(x, y + d, z, k))

    def turn_send_x0(g):
        begin, size = groups[g]
        wait(zb.at[:, pl.ds(begin, size)], y0recv.at[g])
        for n in range(begin, begin + size):
            turned[pl.ds(0, 256), :] = zb[:, n].reshape(256, 128).astype(F32)
            for r in range(8):
                zx[r // 2, n, r % 2] = turned[pl.ds(r, 32, stride=8), :].astype(BF16)
            src = (z + REL[n]) % NZ
            dst = got.at[0, (src // 2) * 2 + k, src % 2, x]
            pltpu.make_async_copy(zx.at[x, n], dst, x0recv.at[n]).start()
            for d in (2, 1, 3):
                remote(zx.at[(x + d) % NX, n], dst, x0send, x0recv.at[n], device(x + d, y, z, k))

    def finish_x0(g):
        begin, size = groups[g]
        for n in range(begin, begin + size):
            wait(slot(0, n), x0recv.at[n])
            forward(0, n)

    rows = vis.shape[2]

    def lay(h, b, q):
        pieces = [got[h, b, zl, xx, q] for xx in range(NX) for zl in range(2)]
        return jnp.concatenate(pieces, axis=0)

    def lay_left(h):
        mine = (z // 2) * 2 + k
        for q in range(2):
            block = lay(h, mine, q)
            left[pl.ds(0, rows), pl.ds(q * 128, 128)] = block
            left[pl.ds(rows, rows), pl.ds((1 - q) * 128, 128)] = block if q else -block

    def multiply(h, b, start, end):
        right = jnp.concatenate([lay(h, b, 0), lay(h, b, 1)], axis=1)
        block = lax.dot_general(left[...], right, NT, preferred_element_type=F32).reshape(2, rows, rows)
        columns = pl.ds(pl.multiple_of(b * rows, rows), rows)
        if not start:
            block = vis[0, :, :, columns] + block
        vis[0, :, :, columns] = block * scale if end else block

    def wait_sibling(h, g):
        begin, size = groups[g]
        wait(got.at[h, pl.ds(begin, size), 0], crecv.at[h, g])

    def correlate(h, start=False):
        if h:
            wait(slot(h, 0), own.at[h])
        wait_sibling(h, 0)
        wait_sibling(h, 1)
        lay_left(h)

        def step(b, _):
            multiply(h, b, start, False)
            return 0

        lax.fori_loop(0, 8, step, 0)

    def correlate_last(h):
        side = 2 * (z % 2) - 1
        tiles = ((z // 2) % 4, (z // 2 + side) % 4, (z // 2 - side) % 4, (z // 2 + 2) % 4)
        wait(slot(h, 0), own.at[h])
        lay_left(h)
        for t in tiles[:2]:
            multiply(h, t * 2 + k, False, True)
        wait_sibling(h, 0)
        for t in tiles[:2]:
            multiply(h, t * 2 + 1 - k, False, True)
        finish_z(h)
        for t in tiles[2:]:
            multiply(h, t * 2 + k, False, True)
        wait_sibling(h, 1)
        for t in tiles[2:]:
            multiply(h, t * 2 + 1 - k, False, True)

    spectra_first()
    pl.semaphore_wait(barrier, len(partners))
    spread(0, first.at[z % 2], first.at[1 - z % 2], at_first)
    spectra(1)
    send_y(1)
    spectra(2)
    spectra(3)
    relay(0, at_first)
    turn(1)
    send_x(1)
    send_y(2)
    wait(za.at[0], own.at[0])
    send_y0(0)
    send_z(1)
    for n in range(5, 8):
        wait(za.at[n], zrecv.at[0, n])
    send_y0(1)
    turn(2)
    send_x(2)
    send_y(3)
    relay_z(1)
    send_z(2)
    turn_send_x0(0)
    turn(3)
    send_x(3)
    finish_z(1)
    send_z(3)
    relay_z(2)
    turn_send_x0(1)
    correlate(1, start=True)
    finish_x0(0)
    finish_z(2)
    relay_z(3)
    finish_x0(1)
    correlate(2)
    correlate(0)
    correlate_last(3)

    wait(got.at[:, pl.ds(0, 4)], csend)
    wait(got.at[:, pl.ds(0, 7), 0], zsend)
    wait(spec.at[:, pl.ds(0, NY - 1)], ysend)
    wait(xs.at[:, pl.ds(0, NX - 1)], xsend)
    wait(za.at[pl.ds(0, NY - 1)], y0send)
    wait(zx.at[pl.ds(0, NX - 1)], x0send)


def per_device(samples, filter_taps, kept_channels, input_flags):
    taps, points = filter_taps.shape
    inputs, length = samples.shape[1:]
    count = length // points - taps + 1
    channels = kept_channels.shape[0]
    vmem, hbm = pl.BlockSpec(memory_space=pltpu.VMEM), pl.BlockSpec(memory_space=pltpu.HBM)
    dma = pltpu.SemaphoreType.DMA
    rows = 256
    late = CH - 1
    operands = (samples, filter_taps, kept_channels.reshape(1, channels), input_flags, jnp.asarray(twiddles(points)))

    return pl.pallas_call(
        functools.partial(body, 1.0 / count),
        out_shape=jax.ShapeDtypeStruct((1, 2, rows, 8 * rows), F32),
        in_specs=[hbm] * 5,
        out_specs=vmem,
        scratch_shapes=[
            *(pltpu.VMEM(a.shape, a.dtype) for a in operands),
            pltpu.VMEM((2, 2, 2 * channels, points), BF16),
            pltpu.VMEM((length // 128 * inputs, 128), F32),
            pltpu.VMEM((2, NY, 2, 16, 128), BF16),
            pltpu.VMEM((late, NY, inputs, 16, 128), BF16),
            pltpu.VMEM((late, NY, inputs, 16, 128), BF16),
            pltpu.VMEM((NY * inputs * 16, 128), F32),
            pltpu.VMEM((late, NX, 2, 2, 32, 128), BF16),
            pltpu.VMEM((late, NX, 2, 2, 32, 128), BF16),
            pltpu.VMEM((8, NY, 2, 16, 128), BF16),
            pltpu.VMEM((NY, 8, 2, 16, 128), BF16),
            pltpu.VMEM((NX, 8, 2, 32, 128), BF16),
            pltpu.VMEM((CH, 8, 2, NX, 2, 32, 128), BF16),
            pltpu.VMEM((2 * rows, 256), BF16),
            dma((CH + 4,)),
            dma,
            dma((late,)),
            dma,
            dma((late,)),
            dma,
            dma((CH, 8)),
            dma,
            dma((CH, 2)),
            dma((CH,)),
            dma,
            dma((2,)),
            dma,
            dma((8,)),
        ],
        compiler_params=pltpu.CompilerParams(
            collective_id=0, has_side_effects=True, vmem_limit_bytes=40 << 20
        ),
        name="correlator",
    )(*operands)


def solution(mesh):
    in_specs = (P(("tile", "cores"), "chan", None), P(), P(), P(("tile", "cores"), "chan"))
    out_specs = P("chan", None, ("tile", "cores"), None)
    return jax.shard_map(
        per_device, mesh=mesh, in_specs=in_specs, out_specs=out_specs, check_vma=False
    )
```

```python
import functools
import math

import jax
import jax.numpy as jnp
from jax import lax
from jax.experimental import pallas as pl
from jax.experimental.pallas import tpu as pltpu
from jax.sharding import PartitionSpec as P

MESH = pl.DeviceIdType.MESH
F32, BF16 = jnp.float32, jnp.bfloat16
NX, NY, NZ = 4, 8, 8
UNROLL = 4
CH = 4
NT = (((1,), (1,)), ((), ()))
REL = (0, -1, 1, -2, 2, -3, 3, 4)


def place():
    chan, tile, core = lax.axis_index("chan"), lax.axis_index("tile"), lax.axis_index("cores")
    return chan // (2 * NY), chan % NY, tile * 2 + (chan // NY) % 2, core


def device(x, y, z, core):
    x, y, z = x % NX, y % NY, z % NZ
    return ((x * 2 + z % 2) * NY + y, z // 2, core)


def body(
    scale, samples, small, vis,
    table, wide, spec, yr, turned, xs, held, za, zb, zx, got, left,
    ysend, yrecv, xsend, xrecv, zsend, zrecv, csend, crecv, own, y0send, y0recv, x0send, x0recv,
):
    x, y, z, k = place()
    inputs, points, count = samples.shape[1], small.shape[1], small.shape[0] - 2
    chunk_blocks, extra = 256, 2 * (count - 1)

    def wait(ref, sem):
        pltpu.make_async_copy(ref, ref, sem).wait()

    def remote(src, dst, ssem, rsem, dev):
        pltpu.make_async_remote_copy(
            src_ref=src, dst_ref=dst, send_sem=ssem, recv_sem=rsem, device_id=dev, device_id_type=MESH
        ).start()

    sib = device(x, y, z, 1 - k)
    barrier = pltpu.get_barrier_semaphore()
    partners = [device(x, y + d, z, k) for d in range(1, NY)]
    partners += [device(x + d, y, z, k) for d in range(1, NX)]
    partners += [device(x, y, z + d, k) for d in (1, 2, NZ - 1, NZ - 2)] + [sib]
    for d in partners:
        pl.semaphore_signal(barrier, inc=1, device_id=d, device_id_type=MESH)

    height, channels = table.shape[1], table.shape[1] // 2
    row = lax.broadcasted_iota(jnp.int32, (height, channels), 0)
    origin = (((row >> 1) & 3) * 2 + (row >> 6)) * NY + ((row >> 3) & 7)
    select = (origin == lax.broadcasted_iota(jnp.int32, row.shape, 1)).astype(F32).astype(BF16)
    kept = jnp.broadcast_to(small[pl.ds(count, 1), pl.ds(0, channels)], (points, channels)).astype(BF16)
    channel = lax.dot_general(select, kept, NT, preferred_element_type=F32).astype(jnp.int32)
    sample = lax.broadcasted_iota(jnp.int32, (height, points), 1)
    quarter = (lax.broadcasted_iota(jnp.int32, (height, points), 0) & 1) * (points // 4)
    turn_at = ((channel * sample + quarter + points // 2) & (points - 1)) - points // 2
    angle = turn_at.astype(F32) * (math.pi / points)
    square = angle * angle
    series = jnp.full(square.shape, 1.0 / math.factorial(13), F32)
    for order in (11, 9, 7, 5, 3, 1):
        series = (-1) ** (order // 2) / math.factorial(order) + square * series
    sine = angle * series
    whole = (1.0 - 2.0 * sine * sine) * (1.0 / math.sqrt(points))
    table[0] = whole.astype(BF16)
    table[1] = (whole - table[0].astype(F32)).astype(BF16)

    stride = 2 * inputs

    def widen(h):
        start = 0 if h == 0 else h * chunk_blocks + extra
        size = chunk_blocks + (extra if h == 0 else 0)
        unroll = 16 if size % 16 == 0 else 2

        def step(s, _):
            for u in range(unroll):
                block = start + s * unroll + u
                values = samples[0, :, pl.ds(pl.multiple_of(block * 128, 128), 128)].astype(F32)
                wide[pl.ds(pl.multiple_of(block * inputs, inputs), inputs), :] = values
            return 0

        lax.fori_loop(0, size // unroll, step, 0)

    def transform(h, i):
        halves = []
        for half in range(2):
            total = None
            for t in range(count):
                rows = wide[pl.ds((h * 128 + t) * stride + half * inputs + i, 128, stride=stride), :]
                term = small[pl.ds(t, 1), pl.ds(half * 128, 128)] * rows
                total = term if total is None else total + term
            halves.append(total)
        filtered = jnp.concatenate(halves, axis=1)
        high = filtered.astype(BF16)
        low = (filtered - high.astype(F32)).astype(BF16)
        spectrum = lax.dot_general(table[0], high, NT, preferred_element_type=F32)
        spectrum += lax.dot_general(table[0], low, NT, preferred_element_type=F32)
        spectrum += lax.dot_general(table[1], high, NT, preferred_element_type=F32)
        return spectrum * small[pl.ds(count + 1, 1), pl.ds(i, 1)]

    def spectra(h):
        widen(h)
        for m in range(inputs // 2):
            pair = [transform(h, 2 * m + i).reshape(2, NY, 8, 128) for i in range(2)]
            spec[h, :, :, m] = jnp.concatenate(pair, axis=2).astype(BF16)

    def send_y(h):
        pltpu.make_async_copy(spec.at[h, :, y], yr.at[h - 1, :, y], yrecv.at[h - 1]).start()
        for d in (4, 3, 5, 2, 6, 1, 7):
            to = (y + d) % NY
            remote(spec.at[h, :, to], yr.at[h - 1, :, y], ysend, yrecv.at[h - 1], device(x, y + d, z, k))

    def wait_y(h):
        wait(yr.at[h - 1], yrecv.at[h - 1])

    def turn(block, write):
        turned[...] = block.reshape(turned.shape).astype(F32)
        for r in range(8):
            write(r // 2, r % 2, turned[pl.ds(r, 32, stride=8), :].astype(BF16))

    def send_x(h):
        for p in range(2):

            def write(xc, q, values, p=p):
                xs[h - 2, xc, p, :, pl.ds(q * 128, 128)] = values

            turn(yr[h - 1, p], write)
        pltpu.make_async_copy(xs.at[h - 2, x], held.at[h - 2, x], xrecv.at[h - 2]).start()
        for d in (2, 1, 3):
            to = (x + d) % NX
            remote(xs.at[h - 2, to], held.at[h - 2, x], xsend, xrecv.at[h - 2], device(x + d, y, z, k))

    def slot(h, n):
        src = (z + REL[n]) % NZ
        return got.at[h, (src // 2) * 2 + k, :, src % 2]

    def forward(h, n):
        remote(slot(h, n), slot(h, n), csend, crecv.at[h, n // 5], sib)

    def spread(h, same, other, at):
        spread_odd(h, other, at)
        spread_even(h, same, at)

    def spread_odd(h, other, at):
        remote(other, at(0, 1), zsend, zrecv.at[h, 1], device(x, y, z + 1, k))
        remote(other, at(0, 2), zsend, zrecv.at[h, 2], device(x, y, z - 1, k))

    def spread_even(h, same, at):
        remote(same, at(0, 3), zsend, zrecv.at[h, 3], device(x, y, z + 2, k))
        remote(same, at(0, 4), zsend, zrecv.at[h, 4], device(x, y, z - 2, k))
        pltpu.make_async_copy(same, at(0, 0), own.at[h]).start()

    def relay(h, at):
        relay_odd(h, at)
        relay_even(h, at)

    def relay_odd(h, at):
        wait(at(1, 1), zrecv.at[h, 1])
        remote(at(1, 1), at(1, 5), zsend, zrecv.at[h, 5], device(x, y, z + 2, k))
        wait(at(2, 2), zrecv.at[h, 2])
        remote(at(2, 2), at(2, 6), zsend, zrecv.at[h, 6], device(x, y, z - 2, k))

    def relay_even(h, at):
        sign = (h + k) % 2
        wait(at(3, 3), zrecv.at[h, 3])
        wait(at(4, 4), zrecv.at[h, 4])
        remote(at(3 + sign, 3 + sign), at(3 + sign, 7), zsend, zrecv.at[h, 7], device(x, y, z + 2 - 4 * sign, k))

    def at_early(h):
        def at(_, n):
            return za.at[h, n]

        return at

    def at_slot(h):
        def at(n, _):
            if isinstance(n, int):
                return slot(h, n)
            src = (z - 2 + 4 * (n - 3)) % NZ
            return got.at[h, (src // 2) * 2 + k, :, src % 2]

        return at

    def spread_early(h):
        spread(h, yr.at[0, z % 2], yr.at[0, 1 - z % 2], at_early(h))

    def relay_early(h):
        relay(h, at_early(h))
        wait(za.at[h, 0], own.at[h])

    def finish_early(h):
        for n in range(5, 8):
            wait(za.at[h, n], zrecv.at[h, n])

    def send_z(h):
        wait(held.at[h - 2], xrecv.at[h - 2])
        same, other = held.at[h - 2, :, z % 2], held.at[h - 2, :, 1 - z % 2]
        spread(h, same, other, at_slot(h))
        remote(same, slot(h, 0), csend, crecv.at[h, 0], sib)

    def relay_z(h):
        relay(h, at_slot(h))
        for n in range(1, 5):
            forward(h, n)

    def finish_z(h):
        for n in range(5, 8):
            wait(slot(h, n), zrecv.at[h, n])
            forward(h, n)

    groups = ((0, 5), (5, 3))

    def send_y0(g):
        begin, size = groups[g]
        mine = pl.ds(begin, size)
        pltpu.make_async_copy(za.at[0, mine, y], zb.at[y, mine], y0recv.at[g]).start()
        for d in (4, 3, 5, 2, 6, 1, 7):
            to = (y + d) % NY
            remote(za.at[0, mine, to], zb.at[y, mine], y0send, y0recv.at[g], device(x, y + d, z, k))

    def send_x_late(h, g):
        begin, size = groups[g]
        if h == 0:
            wait(zb.at[:, pl.ds(begin, size)], y0recv.at[g])
        for n in range(begin, begin + size):

            def write(xc, q, values, n=n):
                zx[h, xc, n, :, pl.ds(q * 128, 128)] = values

            turn(za[1, n] if h else zb[:, n], write)
            src = (z + REL[n]) % NZ
            dst = got.at[h, (src // 2) * 2 + k, x, src % 2]
            pltpu.make_async_copy(zx.at[h, x, n], dst, x0recv.at[h, n]).start()
            for d in (2, 1, 3):
                remote(zx.at[h, (x + d) % NX, n], dst, x0send, x0recv.at[h, n], device(x + d, y, z, k))

    def finish_x_late(h, g):
        begin, size = groups[g]
        for n in range(begin, begin + size):
            wait(slot(h, n), x0recv.at[h, n])
            forward(h, n)

    rows = vis.shape[2]

    def lay(h, b):
        return got[h, b].reshape(rows, 256)

    def lay_left(h):
        block = lay(h, (z // 2) * 2 + k)
        left[h, pl.ds(0, rows)] = block
        left[h, pl.ds(rows, rows), pl.ds(0, 128)] = block[:, 128:]
        left[h, pl.ds(rows, rows), pl.ds(128, 128)] = -block[:, :128]

    def product(h, b):
        return lax.dot_general(left[h], lay(h, b), NT, preferred_element_type=F32).reshape(2, rows, rows)

    def columns(b):
        return pl.ds(pl.multiple_of(b * rows, rows), rows)

    def wait_sibling(h, g):
        begin, size = groups[g]
        wait(got.at[h, pl.ds(begin, size), :, 0], crecv.at[h, g])

    def correlate(h, start=False):
        if h > 1:
            wait(slot(h, 0), own.at[h])
        wait_sibling(h, 0)
        wait_sibling(h, 1)
        lay_left(h)

        def step(b, _):
            vis[0, :, :, columns(b)] = product(h, b) if start else vis[0, :, :, columns(b)] + product(h, b)
            return 0

        lax.fori_loop(0, 8, step, 0, unroll=UNROLL)

    def multiply(h, b):
        vis[0, :, :, columns(b)] = (vis[0, :, :, columns(b)] + product(h, b)) * scale

    def correlate_last(h):
        side = 2 * (z % 2) - 1
        tiles = ((z // 2) % 4, (z // 2 + side) % 4, (z // 2 - side) % 4, (z // 2 + 2) % 4)
        wait(slot(h, 0), own.at[h])
        lay_left(h)
        for t in tiles:
            multiply(h, t * 2 + k)
        wait_sibling(h, 0)
        for t in tiles[:2]:
            multiply(h, t * 2 + 1 - k)
        wait_sibling(h, 1)
        for t in tiles[2:]:
            multiply(h, t * 2 + 1 - k)

    spectra(0)
    pl.semaphore_wait(barrier, len(partners))
    spread_odd(0, spec.at[0, 1 - z % 2], at_early(0))
    spectra(1)
    spread_even(0, spec.at[0, z % 2], at_early(0))
    send_y(1)
    spectra(2)
    send_y(2)
    relay_odd(0, at_early(0))
    spectra(3)
    send_y(3)
    relay_even(0, at_early(0))
    wait(za.at[0, 0], own.at[0])
    wait_y(1)
    spread_early(1)
    wait_y(2)
    send_x(2)
    send_y0(0)
    wait_y(3)
    send_x(3)
    send_z(2)
    finish_early(0)
    send_y0(1)
    relay_early(1)
    send_x_late(1, 0)
    send_z(3)
    relay_z(2)
    finish_early(1)
    send_x_late(1, 1)
    send_x_late(0, 0)
    relay_z(3)
    send_x_late(0, 1)
    finish_x_late(1, 0)
    finish_x_late(1, 1)
    finish_x_late(0, 0)
    correlate(1, start=True)
    finish_x_late(0, 1)
    finish_z(2)
    correlate(0)
    finish_z(3)
    correlate(2)
    correlate_last(3)

    wait(got.at[:, pl.ds(0, 4)], csend)
    wait(got.at[:, pl.ds(0, 7), :, 0], zsend)
    wait(spec.at[pl.ds(0, CH - 1), :, pl.ds(0, NY - 1)], ysend)
    wait(xs.at[:, pl.ds(0, NX - 1)], xsend)
    wait(za.at[0, pl.ds(0, NY - 1)], y0send)
    wait(zx.at[:, pl.ds(0, NX - 1)], x0send)


def per_device(samples, filter_taps, kept_channels, input_flags):
    count, points = filter_taps.shape
    inputs, length = samples.shape[1:]
    spectra = length // points - count + 1
    channels = kept_channels.shape[0]
    vmem = pl.BlockSpec(memory_space=pltpu.VMEM)
    dma = pltpu.SemaphoreType.DMA
    rows = 256
    late = CH - 1
    def lengthen(values):
        return jnp.pad(values, ((0, 0), (0, points - values.shape[1]))).astype(F32)

    small = jnp.concatenate([filter_taps, lengthen(kept_channels[None]), lengthen(input_flags)])

    return pl.pallas_call(
        functools.partial(body, 1.0 / spectra),
        out_shape=jax.ShapeDtypeStruct((1, 2, rows, 8 * rows), F32),
        in_specs=[vmem] * 2,
        out_specs=vmem,
        scratch_shapes=[
            pltpu.VMEM((2, 2 * channels, points), BF16),
            pltpu.VMEM((length // 128 * inputs, 128), F32),
            pltpu.VMEM((CH, 2, NY, 2, 16, 128), BF16),
            pltpu.VMEM((late, 2, NY, 2, 16, 128), BF16),
            pltpu.VMEM((NY * inputs * 8, 128), F32),
            pltpu.VMEM((2, NX, 2, 32, 256), BF16),
            pltpu.VMEM((2, NX, 2, 32, 256), BF16),
            pltpu.VMEM((2, 8, NY, 2, 16, 128), BF16),
            pltpu.VMEM((NY, 8, 2, 16, 128), BF16),
            pltpu.VMEM((2, NX, 8, 32, 256), BF16),
            pltpu.VMEM((CH, 8, NX, 2, 32, 256), BF16),
            pltpu.VMEM((CH, 2 * rows, 256), BF16),
            dma,
            dma((late,)),
            dma,
            dma((2,)),
            dma,
            dma((CH, 8)),
            dma,
            dma((CH, 2)),
            dma((CH,)),
            dma,
            dma((2,)),
            dma,
            dma((2, 8)),
        ],
        compiler_params=pltpu.CompilerParams(
            collective_id=0, has_side_effects=True, vmem_limit_bytes=40 << 20
        ),
        name="correlator",
    )(samples, small)


def solution(mesh):
    in_specs = (P(("tile", "cores"), "chan", None), P(), P(), P(("tile", "cores"), "chan"))
    out_specs = P("chan", None, ("tile", "cores"), None)
    return jax.shard_map(
        per_device, mesh=mesh, in_specs=in_specs, out_specs=out_specs, check_vma=False
    )
```

```python
import functools
import math

import jax
import jax.numpy as jnp
from jax import lax
from jax.experimental import pallas as pl
from jax.experimental.pallas import tpu as pltpu
from jax.sharding import PartitionSpec as P

MESH = pl.DeviceIdType.MESH
F32, BF16 = jnp.float32, jnp.bfloat16
NX, NY, NZ = 4, 8, 8
UNROLL = 4
CH = 4
NT = (((1,), (1,)), ((), ()))
REL = (0, -1, 1, -2, 2, -3, 3, 4)


def place():
    chan, tile, core = lax.axis_index("chan"), lax.axis_index("tile"), lax.axis_index("cores")
    return chan // (2 * NY), chan % NY, tile * 2 + (chan // NY) % 2, core


def device(x, y, z, core):
    x, y, z = x % NX, y % NY, z % NZ
    return ((x * 2 + z % 2) * NY + y, z // 2, core)


def body(
    scale, samples_hbm, taps_hbm, kept_hbm, flags_hbm, vis,
    samples, taps, kept, flags, load, table, wide, spec, yr, turned, xs, held, za, zb, zx, got, left,
    ysend, yrecv, xsend, xrecv, zsend, zrecv, csend, crecv, own, y0send, y0recv, x0send, x0recv,
):
    x, y, z, k = place()
    inputs, (count, points) = samples.shape[1], taps.shape
    chunk_blocks, extra = 256, 2 * (count - 1)

    def wait(ref, sem):
        pltpu.make_async_copy(ref, ref, sem).wait()

    def remote(src, dst, ssem, rsem, dev):
        pltpu.make_async_remote_copy(
            src_ref=src, dst_ref=dst, send_sem=ssem, recv_sem=rsem, device_id=dev, device_id_type=MESH
        ).start()

    def piece(h):
        start = 0 if h == 0 else h * chunk_blocks + extra
        return start, chunk_blocks + (extra if h == 0 else 0)

    loads = [
        pltpu.make_async_copy(src, dst, load.at[CH + n])
        for n, (src, dst) in enumerate(((kept_hbm, kept), (taps_hbm, taps), (flags_hbm, flags)))
    ]
    for h in range(CH):
        start, size = piece(h)
        where = (slice(None), slice(None), pl.ds(start * 128, size * 128))
        loads.append(pltpu.make_async_copy(samples_hbm.at[where], samples.at[where], load.at[h]))
    for copy in loads:
        copy.start()

    sib = device(x, y, z, 1 - k)
    barrier = pltpu.get_barrier_semaphore()
    partners = [device(x, y + d, z, k) for d in range(1, NY)]
    partners += [device(x + d, y, z, k) for d in range(1, NX)]
    partners += [device(x, y, z + d, k) for d in (1, 2, NZ - 1, NZ - 2)] + [sib]
    for d in partners:
        pl.semaphore_signal(barrier, inc=1, device_id=d, device_id_type=MESH)

    for copy in loads[:3]:
        copy.wait()

    height, channels = table.shape[1], table.shape[1] // 2
    row = lax.broadcasted_iota(jnp.int32, (height, channels), 0)
    origin = (((row >> 1) & 3) * 2 + (row >> 6)) * NY + ((row >> 3) & 7)
    select = (origin == lax.broadcasted_iota(jnp.int32, row.shape, 1)).astype(F32).astype(BF16)
    spread_kept = jnp.broadcast_to(kept[...].astype(F32), (points, channels)).astype(BF16)
    channel = lax.dot_general(select, spread_kept, NT, preferred_element_type=F32).astype(jnp.int32)
    sample = lax.broadcasted_iota(jnp.int32, (height, points), 1)
    quarter = (lax.broadcasted_iota(jnp.int32, (height, points), 0) & 1) * (points // 4)
    turn_at = ((channel * sample + quarter + points // 2) & (points - 1)) - points // 2
    angle = turn_at.astype(F32) * (math.pi / points)
    square = angle * angle
    series = jnp.full(square.shape, 1.0 / math.factorial(13), F32)
    for order in (11, 9, 7, 5, 3, 1):
        series = (-1) ** (order // 2) / math.factorial(order) + square * series
    sine = angle * series
    whole = (1.0 - 2.0 * sine * sine) * (1.0 / math.sqrt(points))
    table[0] = whole.astype(BF16)
    table[1] = (whole - table[0].astype(F32)).astype(BF16)

    stride = 2 * inputs

    def widen(h):
        loads[3 + h].wait()
        start, size = piece(h)
        unroll = 16 if size % 16 == 0 else 2

        def step(s, _):
            for u in range(unroll):
                block = start + s * unroll + u
                values = samples[0, :, pl.ds(pl.multiple_of(block * 128, 128), 128)].astype(F32)
                wide[pl.ds(pl.multiple_of(block * inputs, inputs), inputs), :] = values
            return 0

        lax.fori_loop(0, size // unroll, step, 0)

    def transform(h, i):
        halves = []
        for half in range(2):
            total = None
            for t in range(count):
                rows = wide[pl.ds((h * 128 + t) * stride + half * inputs + i, 128, stride=stride), :]
                term = taps[pl.ds(t, 1), pl.ds(half * 128, 128)] * rows
                total = term if total is None else total + term
            halves.append(total)
        filtered = jnp.concatenate(halves, axis=1)
        high = filtered.astype(BF16)
        low = (filtered - high.astype(F32)).astype(BF16)
        spectrum = lax.dot_general(table[0], high, NT, preferred_element_type=F32)
        spectrum += lax.dot_general(table[0], low, NT, preferred_element_type=F32)
        spectrum += lax.dot_general(table[1], high, NT, preferred_element_type=F32)
        return spectrum * flags[pl.ds(0, 1), pl.ds(i, 1)].astype(F32)

    def spectra(h):
        widen(h)
        for m in range(inputs // 2):
            pair = [transform(h, 2 * m + i).reshape(2, NY, 8, 128) for i in range(2)]
            spec[h, :, :, m] = jnp.concatenate(pair, axis=2).astype(BF16)

    def send_y(h):
        pltpu.make_async_copy(spec.at[h, :, y], yr.at[h - 1, :, y], yrecv.at[h - 1]).start()
        for d in (4, 3, 5, 2, 6, 1, 7):
            to = (y + d) % NY
            remote(spec.at[h, :, to], yr.at[h - 1, :, y], ysend, yrecv.at[h - 1], device(x, y + d, z, k))

    def wait_y(h):
        wait(yr.at[h - 1], yrecv.at[h - 1])

    def turn(block, write):
        turned[...] = block.reshape(turned.shape).astype(F32)
        for r in range(8):
            write(r // 2, r % 2, turned[pl.ds(r, 32, stride=8), :].astype(BF16))

    def send_x(h):
        for p in range(2):

            def write(xc, q, values, p=p):
                xs[h - 2, xc, p, :, pl.ds(q * 128, 128)] = values

            turn(yr[h - 1, p], write)
        pltpu.make_async_copy(xs.at[h - 2, x], held.at[h - 2, x], xrecv.at[h - 2]).start()
        for d in (2, 1, 3):
            to = (x + d) % NX
            remote(xs.at[h - 2, to], held.at[h - 2, x], xsend, xrecv.at[h - 2], device(x + d, y, z, k))

    def slot(h, n):
        src = (z + REL[n]) % NZ
        return got.at[h, (src // 2) * 2 + k, :, src % 2]

    def forward(h, n):
        remote(slot(h, n), slot(h, n), csend, crecv.at[h, n // 5], sib)

    def spread(h, same, other, at):
        spread_odd(h, other, at)
        spread_even(h, same, at)

    def spread_odd(h, other, at):
        remote(other, at(0, 1), zsend, zrecv.at[h, 1], device(x, y, z + 1, k))
        remote(other, at(0, 2), zsend, zrecv.at[h, 2], device(x, y, z - 1, k))

    def spread_even(h, same, at):
        remote(same, at(0, 3), zsend, zrecv.at[h, 3], device(x, y, z + 2, k))
        remote(same, at(0, 4), zsend, zrecv.at[h, 4], device(x, y, z - 2, k))
        pltpu.make_async_copy(same, at(0, 0), own.at[h]).start()

    def relay(h, at):
        relay_odd(h, at)
        relay_even(h, at)

    def relay_odd(h, at):
        wait(at(1, 1), zrecv.at[h, 1])
        remote(at(1, 1), at(1, 5), zsend, zrecv.at[h, 5], device(x, y, z + 2, k))
        wait(at(2, 2), zrecv.at[h, 2])
        remote(at(2, 2), at(2, 6), zsend, zrecv.at[h, 6], device(x, y, z - 2, k))

    def relay_even(h, at):
        sign = (h + k) % 2
        wait(at(3, 3), zrecv.at[h, 3])
        wait(at(4, 4), zrecv.at[h, 4])
        remote(at(3 + sign, 3 + sign), at(3 + sign, 7), zsend, zrecv.at[h, 7], device(x, y, z + 2 - 4 * sign, k))

    def at_early(h):
        def at(_, n):
            return za.at[h, n]

        return at

    def at_slot(h):
        def at(n, _):
            if isinstance(n, int):
                return slot(h, n)
            src = (z - 2 + 4 * (n - 3)) % NZ
            return got.at[h, (src // 2) * 2 + k, :, src % 2]

        return at

    def spread_early(h):
        spread(h, yr.at[0, z % 2], yr.at[0, 1 - z % 2], at_early(h))

    def relay_early(h):
        relay(h, at_early(h))
        wait(za.at[h, 0], own.at[h])

    def finish_early(h):
        for n in range(5, 8):
            wait(za.at[h, n], zrecv.at[h, n])

    def send_z(h):
        wait(held.at[h - 2], xrecv.at[h - 2])
        same, other = held.at[h - 2, :, z % 2], held.at[h - 2, :, 1 - z % 2]
        spread(h, same, other, at_slot(h))
        remote(same, slot(h, 0), csend, crecv.at[h, 0], sib)

    def relay_z(h):
        relay(h, at_slot(h))
        for n in range(1, 5):
            forward(h, n)

    def finish_z(h):
        for n in range(5, 8):
            wait(slot(h, n), zrecv.at[h, n])
            forward(h, n)

    groups = ((0, 5), (5, 3))

    def send_y0(g):
        begin, size = groups[g]
        mine = pl.ds(begin, size)
        pltpu.make_async_copy(za.at[0, mine, y], zb.at[y, mine], y0recv.at[g]).start()
        for d in (4, 3, 5, 2, 6, 1, 7):
            to = (y + d) % NY
            remote(za.at[0, mine, to], zb.at[y, mine], y0send, y0recv.at[g], device(x, y + d, z, k))

    def send_x_late(h, g):
        begin, size = groups[g]
        if h == 0:
            wait(zb.at[:, pl.ds(begin, size)], y0recv.at[g])
        for n in range(begin, begin + size):

            def write(xc, q, values, n=n):
                zx[h, xc, n, :, pl.ds(q * 128, 128)] = values

            turn(za[1, n] if h else zb[:, n], write)
            src = (z + REL[n]) % NZ
            dst = got.at[h, (src // 2) * 2 + k, x, src % 2]
            pltpu.make_async_copy(zx.at[h, x, n], dst, x0recv.at[h, n]).start()
            for d in (2, 1, 3):
                remote(zx.at[h, (x + d) % NX, n], dst, x0send, x0recv.at[h, n], device(x + d, y, z, k))

    def finish_x_late(h, g):
        begin, size = groups[g]
        for n in range(begin, begin + size):
            wait(slot(h, n), x0recv.at[h, n])
            forward(h, n)

    rows = vis.shape[2]

    def lay(h, b):
        return got[h, b].reshape(rows, 256)

    def lay_left(h):
        block = lay(h, (z // 2) * 2 + k)
        left[h, pl.ds(0, rows)] = block
        left[h, pl.ds(rows, rows), pl.ds(0, 128)] = block[:, 128:]
        left[h, pl.ds(rows, rows), pl.ds(128, 128)] = -block[:, :128]

    def product(h, b):
        return lax.dot_general(left[h], lay(h, b), NT, preferred_element_type=F32).reshape(2, rows, rows)

    def columns(b):
        return pl.ds(pl.multiple_of(b * rows, rows), rows)

    def wait_sibling(h, g):
        begin, size = groups[g]
        wait(got.at[h, pl.ds(begin, size), :, 0], crecv.at[h, g])

    def correlate(h, start=False):
        if h > 1:
            wait(slot(h, 0), own.at[h])
        wait_sibling(h, 0)
        wait_sibling(h, 1)
        lay_left(h)

        def step(b, _):
            vis[0, :, :, columns(b)] = product(h, b) if start else vis[0, :, :, columns(b)] + product(h, b)
            return 0

        lax.fori_loop(0, 8, step, 0, unroll=UNROLL)

    def multiply(chunks, b):
        total = vis[0, :, :, columns(b)]
        for h in chunks:
            total = total + product(h, b)
        vis[0, :, :, columns(b)] = total * scale

    def correlate_last(*chunks):
        wait(slot(CH - 1, 0), own.at[CH - 1])
        for h in chunks:
            lay_left(h)
        for t in range(4):
            multiply(chunks, t * 2 + k)
        for h in chunks:
            wait_sibling(h, 0)
            wait_sibling(h, 1)
        for t in range(4):
            multiply(chunks, t * 2 + 1 - k)

    spectra(0)
    pl.semaphore_wait(barrier, len(partners))
    spread_odd(0, spec.at[0, 1 - z % 2], at_early(0))
    spectra(1)
    spread_even(0, spec.at[0, z % 2], at_early(0))
    send_y(1)
    spectra(2)
    send_y(2)
    relay_odd(0, at_early(0))
    spectra(3)
    send_y(3)
    relay_even(0, at_early(0))
    wait(za.at[0, 0], own.at[0])
    wait_y(1)
    spread_early(1)
    wait_y(2)
    send_x(2)
    send_y0(0)
    wait_y(3)
    send_x(3)
    send_z(2)
    finish_early(0)
    send_y0(1)
    relay_early(1)
    send_x_late(1, 0)
    send_z(3)
    relay_z(2)
    finish_early(1)
    send_x_late(1, 1)
    send_x_late(0, 0)
    relay_z(3)
    send_x_late(0, 1)
    finish_x_late(1, 0)
    finish_x_late(1, 1)
    finish_z(2)
    finish_x_late(0, 0)
    correlate(1, start=True)
    correlate(2)
    finish_x_late(0, 1)
    finish_z(3)
    correlate_last(0, 3)

    wait(got.at[:, pl.ds(0, 4)], csend)
    wait(got.at[:, pl.ds(0, 7), :, 0], zsend)
    wait(spec.at[pl.ds(0, CH - 1), :, pl.ds(0, NY - 1)], ysend)
    wait(xs.at[:, pl.ds(0, NX - 1)], xsend)
    wait(za.at[0, pl.ds(0, NY - 1)], y0send)
    wait(zx.at[:, pl.ds(0, NX - 1)], x0send)


def per_device(samples, filter_taps, kept_channels, input_flags):
    count, points = filter_taps.shape
    inputs, length = samples.shape[1:]
    spectra = length // points - count + 1
    channels = kept_channels.shape[0]
    vmem = pl.BlockSpec(memory_space=pltpu.VMEM)
    dma = pltpu.SemaphoreType.DMA
    rows = 256
    late = CH - 1
    operands = (samples, filter_taps, kept_channels.reshape(1, channels), input_flags)

    return pl.pallas_call(
        functools.partial(body, 1.0 / spectra),
        out_shape=jax.ShapeDtypeStruct((1, 2, rows, 8 * rows), F32),
        in_specs=[pl.BlockSpec(memory_space=pl.ANY)] * 4,
        out_specs=vmem,
        scratch_shapes=[
            *(pltpu.VMEM(a.shape, a.dtype) for a in operands),
            dma((CH + 3,)),
            pltpu.VMEM((2, 2 * channels, points), BF16),
            pltpu.VMEM((length // 128 * inputs, 128), F32),
            pltpu.VMEM((CH, 2, NY, 2, 16, 128), BF16),
            pltpu.VMEM((late, 2, NY, 2, 16, 128), BF16),
            pltpu.VMEM((NY * inputs * 8, 128), F32),
            pltpu.VMEM((2, NX, 2, 32, 256), BF16),
            pltpu.VMEM((2, NX, 2, 32, 256), BF16),
            pltpu.VMEM((2, 8, NY, 2, 16, 128), BF16),
            pltpu.VMEM((NY, 8, 2, 16, 128), BF16),
            pltpu.VMEM((2, NX, 8, 32, 256), BF16),
            pltpu.VMEM((CH, 8, NX, 2, 32, 256), BF16),
            pltpu.VMEM((CH, 2 * rows, 256), BF16),
            dma,
            dma((late,)),
            dma,
            dma((2,)),
            dma,
            dma((CH, 8)),
            dma,
            dma((CH, 2)),
            dma((CH,)),
            dma,
            dma((2,)),
            dma,
            dma((2, 8)),
        ],
        compiler_params=pltpu.CompilerParams(
            collective_id=0, has_side_effects=True, vmem_limit_bytes=40 << 20
        ),
        name="correlator",
    )(*(pltpu.with_memory_space_constraint(a, pltpu.HBM) for a in operands))


def solution(mesh):
    in_specs = (P(("tile", "cores"), "chan", None), P(), P(), P(("tile", "cores"), "chan"))
    out_specs = P("chan", None, ("tile", "cores"), None)
    return jax.shard_map(
        per_device, mesh=mesh, in_specs=in_specs, out_specs=out_specs, check_vma=False
    )
```

```python
import functools
import math

import jax
import jax.numpy as jnp
from jax import lax
from jax.experimental import pallas as pl
from jax.experimental.pallas import tpu as pltpu
from jax.sharding import PartitionSpec as P

MESH = pl.DeviceIdType.MESH
F32, BF16 = jnp.float32, jnp.bfloat16
NX, NY, NZ = 4, 8, 8
UNROLL = 4
CH = 4
NT = (((1,), (1,)), ((), ()))
REL = (0, -1, 1, -2, 2, -3, 3, 4)


def place():
    chan, tile, core = lax.axis_index("chan"), lax.axis_index("tile"), lax.axis_index("cores")
    return chan // (2 * NY), chan % NY, tile * 2 + (chan // NY) % 2, core


def device(x, y, z, core):
    x, y, z = x % NX, y % NY, z % NZ
    return ((x * 2 + z % 2) * NY + y, z // 2, core)


def body(
    scale, samples_hbm, taps_hbm, kept_hbm, flags_hbm, vis,
    samples, taps, kept, flags, load, table, wide, spec, yr, turned, xs, held, za, zb, zx, got, left,
    ysend, yrecv, xsend, xrecv, zsend, zrecv, csend, crecv, own, y0send, y0recv, x0send, x0recv,
):
    x, y, z, k = place()
    inputs, (count, points) = samples.shape[1], taps.shape
    chunk_blocks, extra = 256, 2 * (count - 1)

    def wait(ref, sem):
        pltpu.make_async_copy(ref, ref, sem).wait()

    def remote(src, dst, ssem, rsem, dev):
        pltpu.make_async_remote_copy(
            src_ref=src, dst_ref=dst, send_sem=ssem, recv_sem=rsem, device_id=dev, device_id_type=MESH
        ).start()

    def piece(h):
        start = 0 if h == 0 else h * chunk_blocks + extra
        return start, chunk_blocks + (extra if h == 0 else 0)

    loads = [
        pltpu.make_async_copy(src, dst, load.at[CH + n])
        for n, (src, dst) in enumerate(((kept_hbm, kept), (taps_hbm, taps), (flags_hbm, flags)))
    ]
    for h in range(CH):
        start, size = piece(h)
        where = (slice(None), slice(None), pl.ds(start * 128, size * 128))
        loads.append(pltpu.make_async_copy(samples_hbm.at[where], samples.at[where], load.at[h]))
    for copy in loads:
        copy.start()

    sib = device(x, y, z, 1 - k)
    barrier = pltpu.get_barrier_semaphore()
    partners = [device(x, y + d, z, k) for d in range(1, NY)]
    partners += [device(x + d, y, z, k) for d in range(1, NX)]
    partners += [device(x, y, z + d, k) for d in (1, 2, NZ - 1, NZ - 2)] + [sib]
    for d in partners:
        pl.semaphore_signal(barrier, inc=1, device_id=d, device_id_type=MESH)

    for copy in loads[:3]:
        copy.wait()

    height, channels = table.shape[1], table.shape[1] // 2
    row = lax.broadcasted_iota(jnp.int32, (height, channels), 0)
    origin = (((row >> 1) & 3) * 2 + (row >> 6)) * NY + ((row >> 3) & 7)
    select = (origin == lax.broadcasted_iota(jnp.int32, row.shape, 1)).astype(F32).astype(BF16)
    spread_kept = jnp.broadcast_to(kept[...].astype(F32), (points, channels)).astype(BF16)
    channel = lax.dot_general(select, spread_kept, NT, preferred_element_type=F32).astype(jnp.int32)
    sample = lax.broadcasted_iota(jnp.int32, (height, points), 1)
    quarter = (lax.broadcasted_iota(jnp.int32, (height, points), 0) & 1) * (points // 4)
    turn_at = ((channel * sample + quarter + points // 2) & (points - 1)) - points // 2
    angle = turn_at.astype(F32) * (math.pi / points)
    square = angle * angle
    series = jnp.full(square.shape, 1.0 / math.factorial(13), F32)
    for order in (11, 9, 7, 5, 3, 1):
        series = (-1) ** (order // 2) / math.factorial(order) + square * series
    sine = angle * series
    whole = (1.0 - 2.0 * sine * sine) * (1.0 / math.sqrt(points))
    table[0] = whole.astype(BF16)
    table[1] = (whole - table[0].astype(F32)).astype(BF16)

    stride = 2 * inputs

    def widen(h):
        loads[3 + h].wait()
        start, size = piece(h)
        unroll = 16 if size % 16 == 0 else 2

        def step(s, _):
            for u in range(unroll):
                block = start + s * unroll + u
                values = samples[0, :, pl.ds(pl.multiple_of(block * 128, 128), 128)].astype(F32)
                wide[pl.ds(pl.multiple_of(block * inputs, inputs), inputs), :] = values
            return 0

        lax.fori_loop(0, size // unroll, step, 0)

    def transform(h, i):
        halves = []
        for half in range(2):
            total = None
            for t in range(count):
                rows = wide[pl.ds((h * 128 + t) * stride + half * inputs + i, 128, stride=stride), :]
                term = taps[pl.ds(t, 1), pl.ds(half * 128, 128)] * rows
                total = term if total is None else total + term
            halves.append(total)
        filtered = jnp.concatenate(halves, axis=1)
        high = filtered.astype(BF16)
        low = (filtered - high.astype(F32)).astype(BF16)
        spectrum = lax.dot_general(table[0], high, NT, preferred_element_type=F32)
        spectrum += lax.dot_general(table[0], low, NT, preferred_element_type=F32)
        spectrum += lax.dot_general(table[1], high, NT, preferred_element_type=F32)
        return spectrum * flags[pl.ds(0, 1), pl.ds(i, 1)].astype(F32)

    def spectra(h):
        widen(h)
        for m in range(inputs // 2):
            pair = [transform(h, 2 * m + i).reshape(2, NY, 8, 128) for i in range(2)]
            spec[h, :, :, m] = jnp.concatenate(pair, axis=2).astype(BF16)

    def send_y(h):
        pltpu.make_async_copy(spec.at[h, :, y], yr.at[h - 1, :, y], yrecv.at[h - 1]).start()
        for d in (4, 3, 5, 2, 6, 1, 7):
            to = (y + d) % NY
            remote(spec.at[h, :, to], yr.at[h - 1, :, y], ysend, yrecv.at[h - 1], device(x, y + d, z, k))

    def wait_y(h):
        wait(yr.at[h - 1], yrecv.at[h - 1])

    def turn(block, write):
        turned[...] = block.reshape(turned.shape).astype(F32)
        for r in range(8):
            write(r // 2, r % 2, turned[pl.ds(r, 32, stride=8), :].astype(BF16))

    def send_x(h):
        for p in range(2):

            def write(xc, q, values, p=p):
                xs[h - 2, xc, p, :, pl.ds(q * 128, 128)] = values

            turn(yr[h - 1, p], write)
        pltpu.make_async_copy(xs.at[h - 2, x], held.at[h - 2, x], xrecv.at[h - 2]).start()
        for d in (2, 1, 3):
            to = (x + d) % NX
            remote(xs.at[h - 2, to], held.at[h - 2, x], xsend, xrecv.at[h - 2], device(x + d, y, z, k))

    def slot(h, n):
        src = (z + REL[n]) % NZ
        return got.at[h, (src // 2) * 2 + k, :, src % 2]

    def forward(h, n):
        remote(slot(h, n), slot(h, n), csend, crecv.at[h, n // 5], sib)

    def spread(h, same, other, at):
        spread_odd(h, other, at)
        spread_even(h, same, at)

    def spread_odd(h, other, at):
        remote(other, at(0, 1), zsend, zrecv.at[h, 1], device(x, y, z + 1, k))
        remote(other, at(0, 2), zsend, zrecv.at[h, 2], device(x, y, z - 1, k))

    def spread_even(h, same, at):
        remote(same, at(0, 3), zsend, zrecv.at[h, 3], device(x, y, z + 2, k))
        remote(same, at(0, 4), zsend, zrecv.at[h, 4], device(x, y, z - 2, k))
        pltpu.make_async_copy(same, at(0, 0), own.at[h]).start()

    def relay(h, at):
        relay_odd(h, at)
        relay_even(h, at)

    def relay_odd(h, at):
        wait(at(1, 1), zrecv.at[h, 1])
        remote(at(1, 1), at(1, 5), zsend, zrecv.at[h, 5], device(x, y, z + 2, k))
        wait(at(2, 2), zrecv.at[h, 2])
        remote(at(2, 2), at(2, 6), zsend, zrecv.at[h, 6], device(x, y, z - 2, k))

    def relay_even(h, at):
        sign = (h + k) % 2
        wait(at(3, 3), zrecv.at[h, 3])
        wait(at(4, 4), zrecv.at[h, 4])
        remote(at(3 + sign, 3 + sign), at(3 + sign, 7), zsend, zrecv.at[h, 7], device(x, y, z + 2 - 4 * sign, k))

    def at_early(h):
        def at(_, n):
            return za.at[h, n]

        return at

    def at_slot(h):
        def at(n, _):
            if isinstance(n, int):
                return slot(h, n)
            src = (z - 2 + 4 * (n - 3)) % NZ
            return got.at[h, (src // 2) * 2 + k, :, src % 2]

        return at

    def spread_early(h):
        spread(h, yr.at[0, z % 2], yr.at[0, 1 - z % 2], at_early(h))

    def relay_early(h):
        relay(h, at_early(h))
        wait(za.at[h, 0], own.at[h])

    def finish_early(h):
        for n in range(5, 8):
            wait(za.at[h, n], zrecv.at[h, n])

    def send_z(h):
        wait(held.at[h - 2], xrecv.at[h - 2])
        same, other = held.at[h - 2, :, z % 2], held.at[h - 2, :, 1 - z % 2]
        spread(h, same, other, at_slot(h))
        remote(same, slot(h, 0), csend, crecv.at[h, 0], sib)

    def relay_z(h):
        relay(h, at_slot(h))
        for n in range(1, 5):
            forward(h, n)

    def finish_z(h):
        for n in range(5, 8):
            wait(slot(h, n), zrecv.at[h, n])
            forward(h, n)

    groups = ((0, 5), (5, 3))

    def send_y0(g):
        begin, size = groups[g]
        mine = pl.ds(begin, size)
        pltpu.make_async_copy(za.at[0, mine, y], zb.at[y, mine], y0recv.at[g]).start()
        for d in (4, 3, 5, 2, 6, 1, 7):
            to = (y + d) % NY
            remote(za.at[0, mine, to], zb.at[y, mine], y0send, y0recv.at[g], device(x, y + d, z, k))

    def send_x_late(h, g):
        begin, size = groups[g]
        if h == 0:
            wait(zb.at[:, pl.ds(begin, size)], y0recv.at[g])
        for n in range(begin, begin + size):

            def write(xc, q, values, n=n):
                zx[h, xc, n, :, pl.ds(q * 128, 128)] = values

            turn(za[1, n] if h else zb[:, n], write)
            src = (z + REL[n]) % NZ
            dst = got.at[h, (src // 2) * 2 + k, x, src % 2]
            pltpu.make_async_copy(zx.at[h, x, n], dst, x0recv.at[h, n]).start()
            for d in (2, 1, 3):
                remote(zx.at[h, (x + d) % NX, n], dst, x0send, x0recv.at[h, n], device(x + d, y, z, k))

    def finish_x_late(h, g):
        begin, size = groups[g]
        for n in range(begin, begin + size):
            wait(slot(h, n), x0recv.at[h, n])
            forward(h, n)

    rows = vis.shape[2]

    def lay(h, b):
        return got[h, b].reshape(rows, 256)

    def lay_left(h):
        block = lay(h, (z // 2) * 2 + k)
        left[h, pl.ds(0, rows)] = block
        left[h, pl.ds(rows, rows), pl.ds(0, 128)] = block[:, 128:]
        left[h, pl.ds(rows, rows), pl.ds(128, 128)] = -block[:, :128]

    def product(h, b):
        return lax.dot_general(left[h], lay(h, b), NT, preferred_element_type=F32).reshape(2, rows, rows)

    def columns(b):
        return pl.ds(pl.multiple_of(b * rows, rows), rows)

    def wait_sibling(h, g):
        begin, size = groups[g]
        wait(got.at[h, pl.ds(begin, size), :, 0], crecv.at[h, g])

    def correlate(h, start=False):
        if h > 1:
            wait(slot(h, 0), own.at[h])
        wait_sibling(h, 0)
        wait_sibling(h, 1)
        lay_left(h)

        def step(b, _):
            vis[0, :, :, columns(b)] = product(h, b) if start else vis[0, :, :, columns(b)] + product(h, b)
            return 0

        lax.fori_loop(0, 8, step, 0, unroll=UNROLL)

    def multiply(chunks, b):
        total = vis[0, :, :, columns(b)]
        for h in chunks:
            total = total + product(h, b)
        vis[0, :, :, columns(b)] = total * scale

    def correlate_last(*chunks):
        side = 2 * (z % 2) - 1
        tiles = (z // 2, (z // 2 + side) % 4, (z // 2 - side) % 4, (z // 2 + 2) % 4)
        wait(slot(CH - 1, 0), own.at[CH - 1])
        for h in chunks:
            lay_left(h)
        for t in tiles:
            multiply(chunks, t * 2 + k)
        for h in chunks[:-1]:
            wait_sibling(h, 0)
            wait_sibling(h, 1)
        wait_sibling(chunks[-1], 0)
        for t in tiles[:2]:
            multiply(chunks, t * 2 + 1 - k)
        wait_sibling(chunks[-1], 1)
        for t in tiles[2:]:
            multiply(chunks, t * 2 + 1 - k)

    spectra(0)
    pl.semaphore_wait(barrier, len(partners))
    spread_odd(0, spec.at[0, 1 - z % 2], at_early(0))
    spectra(1)
    spread_even(0, spec.at[0, z % 2], at_early(0))
    send_y(1)
    spectra(2)
    send_y(2)
    relay_odd(0, at_early(0))
    spectra(3)
    send_y(3)
    relay_even(0, at_early(0))
    wait(za.at[0, 0], own.at[0])
    wait_y(1)
    spread_early(1)
    wait_y(2)
    send_x(2)
    send_y0(0)
    wait_y(3)
    send_x(3)
    send_z(2)
    finish_early(0)
    send_y0(1)
    relay_early(1)
    send_z(3)
    send_x_late(1, 0)
    relay_z(2)
    finish_early(1)
    send_x_late(1, 1)
    send_x_late(0, 0)
    relay_z(3)
    send_x_late(0, 1)
    finish_x_late(1, 0)
    finish_x_late(1, 1)
    finish_z(2)
    finish_x_late(0, 0)
    correlate(1, start=True)
    finish_x_late(0, 1)
    finish_z(3)
    correlate(2)
    correlate_last(0, 3)

    wait(got.at[:, pl.ds(0, 4)], csend)
    wait(got.at[:, pl.ds(0, 7), :, 0], zsend)
    wait(spec.at[pl.ds(0, CH - 1), :, pl.ds(0, NY - 1)], ysend)
    wait(xs.at[:, pl.ds(0, NX - 1)], xsend)
    wait(za.at[0, pl.ds(0, NY - 1)], y0send)
    wait(zx.at[:, pl.ds(0, NX - 1)], x0send)


def per_device(samples, filter_taps, kept_channels, input_flags):
    count, points = filter_taps.shape
    inputs, length = samples.shape[1:]
    spectra = length // points - count + 1
    channels = kept_channels.shape[0]
    vmem = pl.BlockSpec(memory_space=pltpu.VMEM)
    dma = pltpu.SemaphoreType.DMA
    rows = 256
    late = CH - 1
    operands = (samples, filter_taps, kept_channels.reshape(1, channels), input_flags)

    return pl.pallas_call(
        functools.partial(body, 1.0 / spectra),
        out_shape=jax.ShapeDtypeStruct((1, 2, rows, 8 * rows), F32),
        in_specs=[pl.BlockSpec(memory_space=pl.ANY)] * 4,
        out_specs=vmem,
        scratch_shapes=[
            *(pltpu.VMEM(a.shape, a.dtype) for a in operands),
            dma((CH + 3,)),
            pltpu.VMEM((2, 2 * channels, points), BF16),
            pltpu.VMEM((length // 128 * inputs, 128), F32),
            pltpu.VMEM((CH, 2, NY, 2, 16, 128), BF16),
            pltpu.VMEM((late, 2, NY, 2, 16, 128), BF16),
            pltpu.VMEM((NY * inputs * 8, 128), F32),
            pltpu.VMEM((2, NX, 2, 32, 256), BF16),
            pltpu.VMEM((2, NX, 2, 32, 256), BF16),
            pltpu.VMEM((2, 8, NY, 2, 16, 128), BF16),
            pltpu.VMEM((NY, 8, 2, 16, 128), BF16),
            pltpu.VMEM((2, NX, 8, 32, 256), BF16),
            pltpu.VMEM((CH, 8, NX, 2, 32, 256), BF16),
            pltpu.VMEM((CH, 2 * rows, 256), BF16),
            dma,
            dma((late,)),
            dma,
            dma((2,)),
            dma,
            dma((CH, 8)),
            dma,
            dma((CH, 2)),
            dma((CH,)),
            dma,
            dma((2,)),
            dma,
            dma((2, 8)),
        ],
        compiler_params=pltpu.CompilerParams(
            collective_id=0, has_side_effects=True, vmem_limit_bytes=40 << 20
        ),
        name="correlator",
    )(*(pltpu.with_memory_space_constraint(a, pltpu.HBM) for a in operands))


def solution(mesh):
    in_specs = (P(("tile", "cores"), "chan", None), P(), P(), P(("tile", "cores"), "chan"))
    out_specs = P("chan", None, ("tile", "cores"), None)
    return jax.shard_map(
        per_device, mesh=mesh, in_specs=in_specs, out_specs=out_specs, check_vma=False
    )
```
